256 devices in a mesh: dp: 32 (over y, z), tensor: 8 (over x, core).
Axes of the slice: x: 4, y: 4, z: 8, core: 2. Of those that a mesh axis runs over, the one named last changes fastest.
Arguments:
- query: bfloat16 [8, 512, 8192], P(None, 'dp', 'tensor'), may hold values from -130 to 130
- new_keys: bfloat16 [8, 512, 1024], P(None, 'dp', 'tensor'), may hold values from -6 to 6
- new_values: bfloat16 [8, 512, 1024], P(None, 'dp', 'tensor'), may hold values from -6 to 6
- cache_keys: bfloat16 [512, 8, 1024, 128], P('dp', 'tensor'), may hold values from -6.5 to 6.5
- cache_values: bfloat16 [512, 8, 1024, 128], P('dp', 'tensor'), may hold values from -6 to 6
- cache_lengths: int32 [512], P('dp'), may hold values from 2 to 1024, as said below
- weight_codes: int32 [8192, 8192], P('tensor', 'dp'), may hold values from -8 to 7
- group_scales: float32 [64, 8192], P('tensor', 'dp'), may hold values from 0.01 to 0.04
Outputs:
- mixed: bfloat16 [8, 512, 8192], P(None, 'tensor', 'dp')
The draws below stay inside these ranges and needn't reach their ends.
Inputs may be any that keep to these rules, and one draw needn't show every extreme that they name: `cache_lengths`: the requests come in blocks of 16 (the requests of one index of dp); in block g every length is at most 2 + 1022 * (g % 4 + 1) // 4, and the block's first request has exactly that length.
All inputs are finite; a program needn't handle non-finite values.
Results may differ from the reference program's by a relative error of at most 0.015.
Values may be sent and summed in bfloat16 or wider, within the bound.
A program may use at most 128 MiB of HBM per device.

```python
import math
import jax
import jax.numpy as jnp
from jax import lax

HEADS = 64
KVH = 8
HD = 128
D = 8192
KV_WIDTH = 1024
GROUP = 128
REQ_DEV = 16
REQUESTS = 512
CACHE = 1024
STEPS = 8


def first_keys(key):
    noise = jax.random.normal(jax.random.fold_in(key, 1), (REQUESTS, KVH, HD), jnp.float32)
    return jnp.clip(noise, -6.0, 6.0)


def draw_cache_keys(key, part):
    first = first_keys(key)
    key = jax.random.fold_in(key, 2)
    base = jnp.clip(jax.random.normal(key, (REQUESTS, KVH, CACHE, HD), jnp.float32), -6.0, 6.0)
    base = base.at[:, :, 0, :].set(first)
    return base.astype(jnp.bfloat16)


def draw_query(key, part):
    key = jax.random.fold_in(key, 3)
    noise = jax.random.normal(key, (STEPS, REQUESTS, HEADS, HD), jnp.float32)
    drawn = jnp.clip(noise, -6.0, 6.0)
    return drawn.reshape(STEPS, REQUESTS, HEADS * HD).astype(jnp.bfloat16)


def draw_cache_lengths(key, part):
    key = jax.random.fold_in(key, 4)
    rows = jnp.arange(REQUESTS, dtype=jnp.int32)
    block = rows // REQ_DEV
    limit = 2 + (CACHE - 2) * (block % 4 + 1) // 4
    raw = jax.random.randint(key, (REQUESTS,), 0, CACHE, dtype=jnp.int32)
    lengths = 2 + raw % (limit - 1)
    return jnp.where(rows % REQ_DEV == 0, limit, lengths).astype(jnp.int32)


def touch_ends(drawn, own_key, smallest, high):
    longest = drawn.shape.index(max(drawn.shape))
    spots = []
    for shift in (0, 1):
        where = [jax.random.randint(jax.random.fold_in(own_key, axis), (), 0, length) for axis, length in enumerate(drawn.shape)]
        where[longest] = (where[longest] + shift) % drawn.shape[longest]
        spots.append(tuple(where))
    return drawn.at[spots[0]].set(smallest).at[spots[1]].set(high)


def steps_of(own_key, extent, pieces, smallest, top_value):
    level, own = 1.0, jax.random.fold_in(own_key, 6)
    for axis_at, blocks in pieces:
        heights = jnp.exp(jax.random.uniform(jax.random.fold_in(own, axis_at), (blocks,), jnp.float32, smallest / len(pieces), top_value / len(pieces)))
        level = level * jnp.repeat(heights, extent[axis_at] // blocks).reshape([-1 if axis == axis_at else 1 for axis in range(len(extent))])
    return level


def normal_values(rng, shape, scale, reach, pieces=(), kind=jnp.bfloat16):
    result = jax.random.normal(rng, shape, jnp.float32) * scale
    if len(pieces) > 0:
        result = steps_of(rng, shape, pieces, -0.22, 0.18) * result
    return jnp.clip(result, min=-reach, max=reach).astype(kind)


def setup_inputs(seed: int = 0) -> dict:
    streams_of = jax.random.split(jax.random.key(seed), 9)
    return {
        "query": draw_query(jax.random.fold_in(streams_of[8], 71), 0),
        "new_keys": normal_values(streams_of[1], (STEPS, REQUESTS, KV_WIDTH), 1.0, 6.0, ((1, 32), (2, 8))),
        "new_values": normal_values(streams_of[2], (STEPS, REQUESTS, KV_WIDTH), 1.0, 6.0, ((1, 32), (2, 8))),
        "cache_keys": draw_cache_keys(jax.random.fold_in(streams_of[8], 71), 0),
        "cache_values": normal_values(streams_of[4], (REQUESTS, KVH, CACHE, HD), 1.0, 6.0, ((0, 32), (1, 8))),
        "cache_lengths": draw_cache_lengths(jax.random.fold_in(streams_of[8], 71), 0),
        "weight_codes": touch_ends(jax.random.randint(streams_of[6], (D, D), -8, 8), jax.random.fold_in(streams_of[6], 1), -8, 7).astype(jnp.int32),
        "group_scales": jnp.clip(jnp.exp(math.log(0.04) - 1.3862944 * jax.random.uniform(streams_of[7], (D // GROUP, D), jnp.float32) ** steps_of(streams_of[7], (D // GROUP, D), ((0, 8), (1, 32)), -0.2, 0.2)), 0.01, 0.04),
    }


def sign_table(order_size):
    line = jnp.arange(order_size, dtype=jnp.int32)
    parity = jnp.zeros((order_size, order_size), jnp.int32)
    for level in range(order_size.bit_length() - 1):
        parity = parity + ((line[:, None] // (2 ** level)) % 2) * ((line[None, :] // (2 ** level)) % 2)
    return (1 - 2 * (parity % 2)).astype(jnp.float32)


def one_request(items):
    query_rows, key_rows, value_rows, cached_keys, cached_values, length = items
    group_size = HEADS // KVH
    scale = HD ** -0.5
    queries = query_rows.astype(jnp.float32).reshape(STEPS, KVH, group_size, HD)
    scores_cache = jnp.einsum('skgd,kcd->skgc', queries, cached_keys.astype(jnp.float32)) * scale
    valid = jnp.arange(CACHE, dtype=jnp.int32) < length
    scores_cache = jnp.where(valid[None, None, None, :], scores_cache, -1e30)
    fresh_keys = key_rows.astype(jnp.float32).reshape(STEPS, KVH, HD)
    scores_new = jnp.einsum('skgd,tkd->skgt', queries, fresh_keys) * scale
    seen = jnp.arange(STEPS)[None, :] <= jnp.arange(STEPS)[:, None]
    scores_new = jnp.where(seen[:, None, None, :], scores_new, -1e30)
    peak_score = jnp.maximum(jnp.max(scores_cache, axis=-1), jnp.max(scores_new, axis=-1))[..., None]
    exp_cache = jnp.exp(scores_cache - peak_score)
    exp_new = jnp.exp(scores_new - peak_score)
    total = jnp.sum(exp_cache, axis=-1, keepdims=True) + jnp.sum(exp_new, axis=-1, keepdims=True)
    probs_cache = (exp_cache / total).astype(jnp.bfloat16)
    probs_new = (exp_new / total).astype(jnp.bfloat16)
    fresh_values = value_rows.astype(jnp.float32).reshape(STEPS, KVH, HD)
    attended = jnp.einsum('skgc,kcd->skgd', probs_cache.astype(jnp.float32), cached_values.astype(jnp.float32))
    attended = attended + jnp.einsum('skgt,tkd->skgd', probs_new.astype(jnp.float32), fresh_values)
    return attended.astype(jnp.bfloat16).reshape(STEPS, D)


def reference(query, new_keys, new_values, cache_keys, cache_values, cache_lengths, weight_codes, group_scales):
    items = (jnp.transpose(query, (1, 0, 2)), jnp.transpose(new_keys, (1, 0, 2)),
             jnp.transpose(new_values, (1, 0, 2)), cache_keys, cache_values, cache_lengths)
    attended = jnp.transpose(lax.map(one_request, items), (1, 0, 2))
    blocks = attended.astype(jnp.float32).reshape(STEPS, REQUESTS, HEADS, HD)
    inner = jnp.einsum('srhd,de->srhe', blocks, sign_table(HD), precision=lax.Precision.HIGHEST)
    outer = jnp.einsum('gh,srhe->srge', sign_table(HEADS), inner, precision=lax.Precision.HIGHEST)
    rotated = (outer.reshape(STEPS * REQUESTS, D) * (D ** -0.5)).astype(jnp.bfloat16)
    wide = rotated.astype(jnp.float32)
    peak = jnp.max(jnp.abs(wide), axis=-1)
    limit = (0.9 * peak)[:, None]
    clipped = jnp.clip(wide, -limit, limit).astype(jnp.bfloat16)
    weight = (weight_codes.astype(jnp.float32).reshape(D // GROUP, GROUP, D) * group_scales[:, None, :]).reshape(D, D).astype(jnp.bfloat16)
    mixed = jnp.dot(clipped, weight, preferred_element_type=jnp.float32)
    return mixed.reshape(STEPS, REQUESTS, D).astype(jnp.bfloat16)
```

```python
import functools

import jax
import jax.numpy as jnp
from jax import lax
from jax.experimental import pallas as pl
from jax.experimental.pallas import tpu as pltpu
from jax.sharding import PartitionSpec as P

MESH = pl.DeviceIdType.MESH
HEADS = 64
KVH = 8
HD = 128
D = 8192
GROUP = 128
STEPS = 8
REQ = 16
CACHE = 1024
NX, NY, NZ = 4, 4, 8
LOG2E = 1.4426950408889634
F32 = jnp.float32
BF16 = jnp.bfloat16


def hadamard(size):
    a = lax.broadcasted_iota(jnp.int32, (size, size), 0)
    b = lax.broadcasted_iota(jnp.int32, (size, size), 1)
    bits = a & b
    bits = bits ^ (bits >> 4)
    bits = bits ^ (bits >> 2)
    bits = bits ^ (bits >> 1)
    return (1 - 2 * (bits & 1)).astype(F32)


def butterfly(values):
    span = 1
    while span < len(values):
        out = list(values)
        for at in range(len(values)):
            if at & span == 0:
                out[at] = values[at] + values[at | span]
                out[at | span] = values[at] - values[at | span]
        values = out
        span *= 2
    return values


def kernel(
    lengths,
    q_hbm,
    nk_hbm,
    nv_hbm,
    k_hbm,
    v_hbm,
    codes_hbm,
    scales_hbm,
    out_ref,
    qb,
    nkb,
    nvb,
    kb,
    vb,
    cb,
    sb,
    qf,
    nkf,
    nvf,
    attf,
    att,
    xb,
    rf,
    yb,
    wb,
    ab,
    pb,
    db,
    eb,
    load_sem,
    k_sem,
    v_sem,
    w_send,
    w_recv,
    wc_send,
    wc_recv,
    x_send,
    x_recv,
    y_send,
    y_recv,
    z_send,
    z_recv,
    p_send,
    p_recv,
    e_send,
    e_recv,
):
    dp = lax.axis_index("dp")
    t = lax.axis_index("tensor")
    x, c = t // 2, t % 2
    y, z = dp // NZ, dp % NZ

    def device(dx=0, core=None, dy=0, dz=0):
        at_x = (x + dx) % NX
        at_c = c if core is None else core
        return (((y + dy) % NY) * NZ + (z + dz) % NZ, at_x * 2 + at_c)

    def peer(offset):
        return (dp, (t + offset) % 8)

    def remote(src, dst, send, recv, to):
        return pltpu.make_async_remote_copy(
            src_ref=src, dst_ref=dst, send_sem=send, recv_sem=recv, device_id=to, device_id_type=MESH
        )

    barrier = pltpu.get_barrier_semaphore()
    partners = (
        [peer(offset) for offset in range(1, 8)]
        + [device(dy=dy) for dy in (1, 2, 3)]
        + [device(dz=dz) for dz in (1, NZ - 1)]
    )
    for to in partners:
        pl.semaphore_signal(barrier, inc=1, device_id=to, device_id_type=MESH)

    loads = [
        pltpu.make_async_copy(src, dst, load_sem.at[n])
        for n, (src, dst) in enumerate(
            ((codes_hbm, cb), (scales_hbm, sb), (q_hbm, qb), (nk_hbm, nkb), (nv_hbm, nvb))
        )
    ]

    def load_k(r):
        return pltpu.make_async_copy(k_hbm.at[r, 0], kb.at[r], k_sem.at[r])

    def load_v(r):
        return pltpu.make_async_copy(v_hbm.at[r, 0], vb.at[r], v_sem.at[r])

    for load in loads:
        load.start()

    def start_loads(r, carry):
        load_k(r).start()
        load_v(r).start()
        return carry

    lax.fori_loop(0, REQ, start_loads, 0)

    loads[0].wait()
    loads[1].wait()
    for group in range(8):
        rows = pl.ds(group * GROUP, GROUP)
        wb[c, 0, rows, :] = (cb[rows, :].astype(F32) * sb[group : group + 1, :]).astype(BF16)
    pl.semaphore_wait(barrier, len(partners))

    half_rows = [pl.ds(0, 512), pl.ds(512, 512)]

    def w_copy(n, src_slot, dst_slot, half, dy):
        return remote(
            wb.at[c, src_slot, half_rows[half]],
            wb.at[c, dst_slot, half_rows[half]],
            w_send.at[n],
            w_recv.at[n],
            device(dy=dy),
        )

    w_right = [w_copy(0, 0, 3, 0, 1), w_copy(1, 0, 3, 1, 1)]
    w_left = [w_copy(2, 0, 1, 0, NY - 1), w_copy(3, 0, 1, 1, NY - 1)]
    w_far = [w_copy(4, 3, 2, 0, 1), w_copy(5, 1, 2, 1, NY - 1)]
    w_right[0].start()
    w_left[1].start()
    w_right[1].start()
    w_left[0].start()

    def w_core(slot):
        return remote(
            wb.at[c, slot], wb.at[c, slot], wc_send.at[slot], wc_recv.at[slot], device(core=1 - c)
        )

    w_core(0).start()

    for load in loads[2:]:
        load.wait()
    for s in range(STEPS):
        for g in range(8):
            qf[pl.ds((s * 8 + g) * REQ, REQ), :] = qb[s, :, g * HD : (g + 1) * HD].astype(F32)
        nkf[pl.ds(s * REQ, REQ), :] = nkb[s].astype(F32)
        nvf[pl.ds(s * REQ, REQ), :] = nvb[s].astype(F32)

    slots = lax.broadcasted_iota(jnp.int32, (64, CACHE), 1)
    new_slot = lax.broadcasted_iota(jnp.int32, (64, HD), 1)
    new_step = lax.broadcasted_iota(jnp.int32, (64, HD), 0) // 8
    seen = new_slot <= new_step
    transposed = (((1,), (1,)), ((), ()))
    rate = LOG2E * HD ** (-0.5)

    def attend(r):
        query = jnp.concatenate(
            [qf[pl.ds(i * 8 * REQ + r, 8, stride=REQ), :] for i in range(8)], axis=0
        ).astype(BF16)
        pad = jnp.zeros((HD - STEPS, HD), F32)
        fresh_k = jnp.concatenate([nkf[pl.ds(r, STEPS, stride=REQ), :], pad], axis=0).astype(BF16)
        fresh_v = jnp.concatenate([nvf[pl.ds(r, STEPS, stride=REQ), :], pad], axis=0).astype(BF16)
        load_k(r).wait()
        old = lax.dot_general(query, kb[r], transposed, preferred_element_type=F32)
        new = lax.dot_general(query, fresh_k, transposed, preferred_element_type=F32)
        old = jnp.where(slots < lengths[r], old, -1e30)
        new = jnp.where(seen, new, -1e30)
        peak = jnp.maximum(
            jnp.max(old, axis=1, keepdims=True), jnp.max(new, axis=1, keepdims=True)
        )
        old = jnp.exp2((old - peak) * rate)
        new = jnp.exp2((new - peak) * rate)
        total = jnp.sum(old, axis=1, keepdims=True) + jnp.sum(new, axis=1, keepdims=True)
        load_v(r).wait()
        result = jnp.dot(old.astype(BF16), vb[r], preferred_element_type=F32)
        result = result + jnp.dot(new.astype(BF16), fresh_v, preferred_element_type=F32)
        result = result / total
        for i in range(8):
            attf[pl.ds(i * 8 * REQ + r, 8, stride=REQ), :] = result[i * 8 : (i + 1) * 8, :]

    def attend_two(n, carry):
        attend(2 * n)
        attend(2 * n + 1)
        return carry

    lax.fori_loop(0, REQ // 2, attend_two, 0)

    for s in range(STEPS):
        for g in range(8):
            att[s, :, g * HD : (g + 1) * HD] = attf[pl.ds((s * 8 + g) * REQ, REQ), :].astype(BF16)

    def x_copy(offset):
        to = peer(offset)
        return remote(att.at[to[1]], xb.at[t], x_send.at[offset], x_recv.at[offset], to)

    for offset in (4, 3, 5, 2, 6, 1, 7):
        x_copy(offset).start()
    xb[t] = att[t]

    w_right[0].wait_recv()
    w_far[0].start()
    w_left[1].wait_recv()
    w_far[1].start()

    for offset in range(1, 8):
        x_copy(offset).wait_recv()

    signs = hadamard(HD).astype(BF16)
    for g in range(8):
        heads = xb[:, :, g * HD : (g + 1) * HD].reshape(8 * REQ, HD)
        rf[g] = jnp.dot(heads, signs, preferred_element_type=F32)
    for kv in range(8):
        rows = pl.ds(kv * REQ, REQ)
        for g, value in enumerate(butterfly([rf[g, rows, :] for g in range(8)])):
            rf[g, rows, :] = value
    top = jnp.zeros((REQ, HD), F32)
    for g in range(8):
        values = butterfly([rf[g, pl.ds(kv * REQ, REQ), :] for kv in range(8)])
        for kv, value in enumerate(values):
            value = (value * D ** (-0.5)).astype(BF16)
            yb[kv // 2, kv % 2, :, g * HD : (g + 1) * HD] = value
            top = jnp.maximum(top, jnp.abs(value.astype(F32)))
    limit = 0.9 * jnp.max(top, axis=1, keepdims=True)
    for kv in range(8):
        value = yb[kv // 2, kv % 2].astype(F32)
        yb[kv // 2, kv % 2] = jnp.clip(value, -limit, limit).astype(BF16)

    row_core = t // 4
    row_slot = t % 4

    def y_copy(dx):
        return remote(
            yb.at[(x + dx) % NX],
            ab.at[0, row_slot],
            y_send.at[dx],
            y_recv.at[row_slot],
            device(dx=dx, core=row_core),
        )

    def y_local():
        return pltpu.make_async_copy(yb.at[x], ab.at[0, row_slot], y_recv.at[row_slot])

    for dx in (2, 1, 3):
        y_copy(dx).start()

    @pl.when(row_core == c)
    def _():
        y_local().start()

    @pl.when(row_core != c)
    def _():
        y_copy(0).start()

    def y_arrived(slot):
        pltpu.make_async_copy(yb.at[0], ab.at[0, slot], y_recv.at[slot]).wait()

    def z_copy(way, d, half):
        src = 0 if d == 1 else (2 * (d - 1) - 1 if way == 0 else 2 * (d - 1))
        dst = 7 if d == 4 else (2 * d - 1 if way == 0 else 2 * d)
        rows = pl.ds(2 * half, 2)
        return remote(
            ab.at[src, rows],
            ab.at[dst, rows],
            z_send.at[way, d - 1, half],
            z_recv.at[way, d - 1, half],
            device(dz=1 if way == 0 else NZ - 1),
        )

    first = [0, 1]

    y_arrived(0)
    y_arrived(1)
    z_copy(0, 1, 0).start()
    z_copy(1, 1, 0).start()
    y_arrived(2)
    y_arrived(3)
    z_copy(0, 1, 1).start()
    z_copy(1, 1, 1).start()

    w_right[1].wait_recv()
    w_core(3).start()
    w_left[0].wait_recv()
    w_core(1).start()
    w_far[0].wait_recv()
    w_far[1].wait_recv()
    w_core(2).start()
    w_core(0).wait_recv()

    spans = [(0, 1), (1, 3), (3, 5), (5, 7), (7, 8)]

    def project(stage, i):
        lo, hi = spans[stage]
        rows = (hi - lo) * 64
        total = jnp.zeros((rows, 256), F32)
        for core in range(2):
            block = ab[lo:hi, :, core].reshape(rows, 1024)
            total = total + jnp.dot(block, wb[core, i], preferred_element_type=F32)
        total = total.astype(BF16).reshape(hi - lo, 64, 256)
        if i == 0:
            db[0, lo:hi] = total
        else:
            pb[i, lo:hi] = total

    def p_copy(stage, i):
        lo, hi = spans[stage]
        at = pl.ds(lo, hi - lo)
        return remote(
            pb.at[i, at], db.at[i, at], p_send.at[stage, i], p_recv.at[stage, i], device(dy=i)
        )

    def z_of(pos):
        dz = 4 if pos == 7 else (NZ - (pos + 1) // 2 if pos % 2 else pos // 2)
        return (z + dz) % NZ

    def e_copy(pos, k):
        block = z_of(pos)
        to_x = (x + k) % NX
        i = (y + NY - to_x) % NY
        return remote(
            db.at[i, pos],
            eb.at[k, c, block % 4],
            e_send.at[k, pos],
            e_recv.at[k, c, block % 4],
            device(dx=k, core=block // 4),
        )

    def e_local(pos):
        block = z_of(pos)
        i = (y + NY - x) % NY
        return pltpu.make_async_copy(
            db.at[i, pos], eb.at[0, c, block % 4], e_recv.at[0, c, block % 4]
        )

    def forward(stage):
        for i in (1, 2, 3):
            p_copy(stage, i).wait_recv()
        for pos in range(*spans[stage]):
            for k in (2, 1, 3):
                e_copy(pos, k).start()
            own = z_of(pos) // 4 == c

            @pl.when(own)
            def _():
                e_local(pos).start()

            @pl.when(jnp.logical_not(own))
            def _():
                e_copy(pos, 0).start()

    for stage in range(5):
        if stage:
            if stage < 4:
                for half in first:
                    for way in range(2):
                        z_copy(way, stage, half).wait_recv()
                        if stage < 3 or half == way:
                            z_copy(way, stage + 1, half).start()
            else:
                z_copy(0, 4, 0).wait_recv()
                z_copy(1, 4, 1).wait_recv()
        for i in (1, 3, 2, 0):
            if stage == 0 and i:
                w_core(i).wait_recv()
            project(stage, i)
            if i:
                p_copy(stage, i).start()
        if stage:
            forward(stage - 1)
    forward(4)

    for zz in range(4):
        for core in range(2):
            for k in range(4):
                pltpu.make_async_copy(
                    db.at[0, 0], eb.at[k, core, zz], e_recv.at[k, core, zz]
                ).wait()
            total = eb[0, core, zz].astype(F32)
            for k in range(1, 4):
                total = total + eb[k, core, zz].astype(F32)
            out_ref[4 * core : 4 * core + 4, zz * REQ : (zz + 1) * REQ, :] = total.astype(
                BF16
            ).reshape(4, REQ, 256)

    for copy in w_right + w_left + w_far:
        copy.wait_send()
    for slot in range(4):
        w_core(slot).wait_send()
    for offset in range(1, 8):
        x_copy(offset).wait_send()
    for dx in (1, 2, 3):
        y_copy(dx).wait_send()

    @pl.when(row_core != c)
    def _():
        y_copy(0).wait_send()

    for d in range(1, 5):
        for half in range(2):
            for way in range(2):
                if d < 4 or half == way:
                    z_copy(way, d, half).wait_send()
    for stage in range(5):
        for i in (1, 2, 3):
            p_copy(stage, i).wait_send()
    for pos in range(8):
        for k in (1, 2, 3):
            e_copy(pos, k).wait_send()

        @pl.when(z_of(pos) // 4 != c)
        def _():
            e_copy(pos, 0).wait_send()


def body(
    query, new_keys, new_values, cache_keys, cache_values, cache_lengths, weight_codes, group_scales
):
    hbm = pl.BlockSpec(memory_space=pl.ANY)
    dma = pltpu.SemaphoreType.DMA
    return pl.pallas_call(
        kernel,
        out_shape=jax.ShapeDtypeStruct((STEPS, 64, 256), BF16),
        in_specs=[pl.BlockSpec(memory_space=pltpu.SMEM)] + [hbm] * 7,
        out_specs=pl.BlockSpec(memory_space=pltpu.VMEM),
        scratch_shapes=[
            pltpu.VMEM((STEPS, REQ, 1024), BF16),
            pltpu.VMEM((STEPS, REQ, HD), BF16),
            pltpu.VMEM((STEPS, REQ, HD), BF16),
            pltpu.VMEM((REQ, CACHE, HD), BF16),
            pltpu.VMEM((REQ, CACHE, HD), BF16),
            pltpu.VMEM((1024, 256), jnp.int32),
            pltpu.VMEM((8, 256), F32),
            pltpu.VMEM((64 * REQ, HD), F32),
            pltpu.VMEM((STEPS * REQ, HD), F32),
            pltpu.VMEM((STEPS * REQ, HD), F32),
            pltpu.VMEM((64 * REQ, HD), F32),
            pltpu.VMEM((STEPS, REQ, 1024), BF16),
            pltpu.VMEM((8, REQ, 1024), BF16),
            pltpu.VMEM((8, 8 * REQ, HD), F32),
            pltpu.VMEM((NX, 2, REQ, 1024), BF16),
            pltpu.VMEM((2, NY, 1024, 256), BF16),
            pltpu.VMEM((8, 4, 2, REQ, 1024), BF16),
            pltpu.VMEM((NY, 8, 64, 256), BF16),
            pltpu.VMEM((NY, 8, 64, 256), BF16),
            pltpu.VMEM((NX, 2, 4, 64, 256), BF16),
            dma((5,)),
            dma((REQ,)),
            dma((REQ,)),
            dma((6,)),
            dma((6,)),
            dma((4,)),
            dma((4,)),
            dma((8,)),
            dma((8,)),
            dma((4,)),
            dma((4,)),
            dma((2, 4, 2)),
            dma((2, 4, 2)),
            dma((5, 4)),
            dma((5, 4)),
            dma((NX, 8)),
            dma((NX, 2, 4)),
        ],
        compiler_params=pltpu.CompilerParams(
            collective_id=0, has_side_effects=True, vmem_limit_bytes=48 << 20
        ),
        name="decode",
    )(
        cache_lengths,
        query,
        new_keys,
        new_values,
        cache_keys,
        cache_values,
        weight_codes,
        group_scales,
    )


def solution(mesh):
    return jax.shard_map(
        body,
        mesh=mesh,
        in_specs=(
            P(None, "dp", "tensor"),
            P(None, "dp", "tensor"),
            P(None, "dp", "tensor"),
            P("dp", "tensor", None, None),
            P("dp", "tensor", None, None),
            P("dp"),
            P("tensor", "dp"),
            P("tensor", "dp"),
        ),
        out_specs=P(None, "tensor", "dp"),
        check_vma=False,
    )
```

```python
import functools

import jax
import jax.numpy as jnp
from jax import lax
from jax.experimental import pallas as pl
from jax.experimental.pallas import tpu as pltpu
from jax.sharding import PartitionSpec as P

MESH = pl.DeviceIdType.MESH
HEADS = 64
KVH = 8
HD = 128
D = 8192
GROUP = 128
STEPS = 8
REQ = 16
CACHE = 1024
NX, NY, NZ = 4, 4, 8
GROUPED = 4
LOG2E = 1.4426950408889634
F32 = jnp.float32
BF16 = jnp.bfloat16


def hadamard(size):
    a = lax.broadcasted_iota(jnp.int32, (size, size), 0)
    b = lax.broadcasted_iota(jnp.int32, (size, size), 1)
    bits = a & b
    bits = bits ^ (bits >> 4)
    bits = bits ^ (bits >> 2)
    bits = bits ^ (bits >> 1)
    return (1 - 2 * (bits & 1)).astype(F32)


def butterfly(values):
    span = 1
    while span < len(values):
        out = list(values)
        for at in range(len(values)):
            if at & span == 0:
                out[at] = values[at] + values[at | span]
                out[at | span] = values[at] - values[at | span]
        values = out
        span *= 2
    return values


def kernel(
    lengths,
    q_hbm,
    nk_hbm,
    nv_hbm,
    k_hbm,
    v_hbm,
    codes_hbm,
    scales_hbm,
    out_ref,
    qb,
    nkb,
    nvb,
    kb,
    vb,
    cb,
    sb,
    qf,
    nkf,
    nvf,
    attf,
    att,
    xb,
    rf,
    yb,
    wb,
    ab,
    pb,
    db,
    eb,
    load_sem,
    k_sem,
    v_sem,
    w_send,
    w_recv,
    wc_send,
    wc_recv,
    x_send,
    x_recv,
    y_send,
    y_recv,
    z_send,
    z_recv,
    p_send,
    p_recv,
    e_send,
    e_recv,
):
    dp = lax.axis_index("dp")
    t = lax.axis_index("tensor")
    x, c = t // 2, t % 2
    y, z = dp // NZ, dp % NZ

    def device(dx=0, core=None, dy=0, dz=0):
        at_x = (x + dx) % NX
        at_c = c if core is None else core
        return (((y + dy) % NY) * NZ + (z + dz) % NZ, at_x * 2 + at_c)

    def peer(offset):
        return (dp, (t + offset) % 8)

    def remote(src, dst, send, recv, to):
        return pltpu.make_async_remote_copy(
            src_ref=src, dst_ref=dst, send_sem=send, recv_sem=recv, device_id=to, device_id_type=MESH
        )

    barrier = pltpu.get_barrier_semaphore()
    partners = (
        [peer(offset) for offset in range(1, 8)]
        + [device(dy=dy) for dy in (1, 2, 3)]
        + [device(dz=dz) for dz in (1, NZ - 1)]
    )
    for to in partners:
        pl.semaphore_signal(barrier, inc=1, device_id=to, device_id_type=MESH)

    loads = [
        pltpu.make_async_copy(src, dst, load_sem.at[n])
        for n, (src, dst) in enumerate(
            ((codes_hbm, cb), (scales_hbm, sb), (q_hbm, qb), (nk_hbm, nkb), (nv_hbm, nvb))
        )
    ]

    def load_k(r):
        return pltpu.make_async_copy(k_hbm.at[r, 0], kb.at[r], k_sem.at[r])

    def load_v(r):
        return pltpu.make_async_copy(v_hbm.at[r, 0], vb.at[r], v_sem.at[r])

    for load in loads:
        load.start()

    def start_loads(r, carry):
        load_k(r).start()
        load_v(r).start()
        return carry

    lax.fori_loop(0, REQ, start_loads, 0)

    loads[0].wait()
    loads[1].wait()
    for group in range(8):
        rows = pl.ds(group * GROUP, GROUP)
        wb[c, 0, rows, :] = (cb[rows, :].astype(F32) * sb[group : group + 1, :]).astype(BF16)
    pl.semaphore_wait(barrier, len(partners))

    half_rows = [pl.ds(0, 512), pl.ds(512, 512)]

    def w_copy(n, src_slot, dst_slot, half, dy):
        return remote(
            wb.at[c, src_slot, half_rows[half]],
            wb.at[c, dst_slot, half_rows[half]],
            w_send.at[n],
            w_recv.at[n],
            device(dy=dy),
        )

    w_right = [w_copy(0, 0, 3, 0, 1), w_copy(1, 0, 3, 1, 1)]
    w_left = [w_copy(2, 0, 1, 0, NY - 1), w_copy(3, 0, 1, 1, NY - 1)]
    w_far = [w_copy(4, 3, 2, 0, 1), w_copy(5, 1, 2, 1, NY - 1)]
    w_right[0].start()
    w_left[1].start()
    w_right[1].start()
    w_left[0].start()

    def w_core(slot):
        return remote(
            wb.at[c, slot], wb.at[c, slot], wc_send.at[slot], wc_recv.at[slot], device(core=1 - c)
        )

    w_core(0).start()

    for load in loads[2:]:
        load.wait()
    for s in range(STEPS):
        for g in range(8):
            qf[pl.ds((s * 8 + g) * REQ, REQ), :] = qb[s, :, g * HD : (g + 1) * HD].astype(F32)
        nkf[pl.ds(s * REQ, REQ), :] = nkb[s].astype(F32)
        nvf[pl.ds(s * REQ, REQ), :] = nvb[s].astype(F32)

    slots = lax.broadcasted_iota(jnp.int32, (64, CACHE), 1)
    new_slot = lax.broadcasted_iota(jnp.int32, (64, HD), 1)
    new_step = lax.broadcasted_iota(jnp.int32, (64, HD), 0) // 8
    seen = new_slot <= new_step
    transposed = (((1,), (1,)), ((), ()))
    rate = LOG2E * HD ** (-0.5)

    def attend(first, count):
        group = [first + n for n in range(count)]
        for r in group:
            load_k(r).wait()
            load_v(r).wait()
        pad = jnp.zeros((HD - STEPS, HD), F32)
        queries = [
            jnp.concatenate(
                [qf[pl.ds(i * 8 * REQ + r, 8, stride=REQ), :] for i in range(8)], axis=0
            ).astype(BF16)
            for r in group
        ]
        fresh_k, fresh_v = (
            [
                jnp.concatenate([ref[pl.ds(r, STEPS, stride=REQ), :], pad], axis=0).astype(BF16)
                for r in group
            ]
            for ref in (nkf, nvf)
        )
        olds = [
            lax.dot_general(query, kb[r], transposed, preferred_element_type=F32)
            for query, r in zip(queries, group)
        ]
        news = [
            lax.dot_general(query, fresh, transposed, preferred_element_type=F32)
            for query, fresh in zip(queries, fresh_k)
        ]
        results = []
        for n, r in enumerate(group):
            old = jnp.where(slots < lengths[r], olds[n], -1e30)
            new = jnp.where(seen, news[n], -1e30)
            peak = jnp.maximum(
                jnp.max(old, axis=1, keepdims=True), jnp.max(new, axis=1, keepdims=True)
            )
            old = jnp.exp2((old - peak) * rate)
            new = jnp.exp2((new - peak) * rate)
            total = jnp.sum(old, axis=1, keepdims=True) + jnp.sum(new, axis=1, keepdims=True)
            result = jnp.dot(old.astype(BF16), vb[r], preferred_element_type=F32)
            result = result + jnp.dot(new.astype(BF16), fresh_v[n], preferred_element_type=F32)
            results.append(result / total)
        for r, result in zip(group, results):
            for i in range(8):
                start = (i // 2) * 8 * REQ + (i % 2) * 8 + r % 8
                attf[r // 8, pl.ds(start, 8, stride=REQ), :] = result[i * 8 : (i + 1) * 8, :]

    def attend_some(n, carry):
        attend(GROUPED * n, GROUPED)
        return carry

    def x_copy(q, offset):
        to = q * 4 + (t + offset) % 4
        return remote(att.at[to], xb.at[t], x_send.at[q, offset], x_recv.at[t], (dp, to))

    def x_local():
        return pltpu.make_async_copy(att.at[t], xb.at[t], x_recv.at[t])

    for q in range(2):
        lax.fori_loop(q * 8 // GROUPED, (q + 1) * 8 // GROUPED, attend_some, 0)
        for u in range(4):
            for g in range(8):
                att[q * 4 + u, :, g * HD : (g + 1) * HD] = attf[
                    q, pl.ds((u * 8 + g) * REQ, REQ), :
                ].astype(BF16)
        for offset in (2, 1, 3):
            x_copy(q, offset).start()

        @pl.when(t // 4 == q)
        def _():
            x_local().start()

        @pl.when(t // 4 != q)
        def _():
            x_copy(q, 0).start()

    w_right[0].wait_recv()
    w_far[0].start()
    w_left[1].wait_recv()
    w_far[1].start()

    for source in range(8):
        pltpu.make_async_copy(att.at[0], xb.at[source], x_recv.at[source]).wait()

    signs = hadamard(HD).astype(BF16)
    for g in range(8):
        heads = xb[:, :, g * HD : (g + 1) * HD].reshape(8 * REQ, HD)
        rf[g] = jnp.dot(heads, signs, preferred_element_type=F32)
    for kv in range(8):
        rows = pl.ds(kv * REQ, REQ)
        for g, value in enumerate(butterfly([rf[g, rows, :] for g in range(8)])):
            rf[g, rows, :] = value
    top = jnp.zeros((REQ, HD), F32)
    for g in range(8):
        values = butterfly([rf[g, pl.ds(kv * REQ, REQ), :] for kv in range(8)])
        for kv, value in enumerate(values):
            value = (value * D ** (-0.5)).astype(BF16)
            yb[kv // 2, kv % 2, :, g * HD : (g + 1) * HD] = value
            top = jnp.maximum(top, jnp.abs(value.astype(F32)))
    limit = 0.9 * jnp.max(top, axis=1, keepdims=True)
    for kv in range(8):
        value = yb[kv // 2, kv % 2].astype(F32)
        yb[kv // 2, kv % 2] = jnp.clip(value, -limit, limit).astype(BF16)

    def y_copy(dx):
        return remote(
            yb.at[(x + dx) % NX], ab.at[0, x], y_send.at[dx], y_recv.at[x], device(dx=dx)
        )

    for dx in (2, 1, 3):
        y_copy(dx).start()
    pltpu.make_async_copy(yb.at[x], ab.at[0, x], y_recv.at[x]).start()

    def y_arrived(slot):
        pltpu.make_async_copy(yb.at[0], ab.at[0, slot], y_recv.at[slot]).wait()

    def z_copy(way, d, half):
        src = 0 if d == 1 else (2 * (d - 1) - 1 if way == 0 else 2 * (d - 1))
        dst = 7 if d == 4 else (2 * d - 1 if way == 0 else 2 * d)
        rows = pl.ds(2 * half, 2)
        return remote(
            ab.at[src, rows],
            ab.at[dst, rows],
            z_send.at[way, d - 1, half],
            z_recv.at[way, d - 1, half],
            device(dz=1 if way == 0 else NZ - 1),
        )

    def z_first(half):
        y_arrived(2 * half)
        y_arrived(2 * half + 1)
        z_copy(0, 1, half).start()
        z_copy(1, 1, half).start()

    spans = [(0, 1), (1, 3), (3, 5), (5, 7), (7, 8)]

    def project(stage, i):
        lo, hi = spans[stage]
        rows = (hi - lo) * 64
        total = jnp.zeros((rows, 256), F32)
        for core in range(2):
            block = ab[lo:hi, :, core].reshape(rows, 1024)
            total = total + jnp.dot(block, wb[core, i], preferred_element_type=F32)
        total = total.astype(BF16).reshape(hi - lo, 64, 256)
        if i == 0:
            db[0, lo:hi] = total
        else:
            pb[i, lo:hi] = total

    def p_copy(stage, i):
        lo, hi = spans[stage]
        at = pl.ds(lo, hi - lo)
        return remote(
            pb.at[i, at], db.at[i, at], p_send.at[stage, i], p_recv.at[stage, i], device(dy=i)
        )

    def z_of(pos):
        dz = 4 if pos == 7 else (NZ - (pos + 1) // 2 if pos % 2 else pos // 2)
        return (z + dz) % NZ

    def e_copy(pos, k):
        block = z_of(pos)
        to_x = (x + k) % NX
        i = (y + NY - to_x) % NY
        return remote(
            db.at[i, pos],
            eb.at[k, c, block % 4],
            e_send.at[k, pos],
            e_recv.at[k, c, block % 4],
            device(dx=k, core=block // 4),
        )

    def e_local(pos):
        block = z_of(pos)
        i = (y + NY - x) % NY
        return pltpu.make_async_copy(
            db.at[i, pos], eb.at[0, c, block % 4], e_recv.at[0, c, block % 4]
        )

    def forward(stage):
        for i in (1, 2, 3):
            p_copy(stage, i).wait_recv()
        for pos in range(*spans[stage]):
            for k in (2, 1, 3):
                e_copy(pos, k).start()
            own = z_of(pos) // 4 == c

            @pl.when(own)
            def _():
                e_local(pos).start()

            @pl.when(jnp.logical_not(own))
            def _():
                e_copy(pos, 0).start()

    def pass_on(d, half):
        for way in range(2):
            z_copy(way, d, half).wait_recv()
            if d < 3 or half == way:
                z_copy(way, d + 1, half).start()

    def multiply(stage):
        for i in (1, 3, 2, 0):
            if stage == 0 and i:
                w_core(i).wait_recv()
            project(stage, i)
            if i:
                p_copy(stage, i).start()

    z_first(0)
    w_right[1].wait_recv()
    w_core(3).start()
    w_left[0].wait_recv()
    w_core(1).start()
    z_first(1)
    pass_on(1, 0)
    w_far[0].wait_recv()
    w_far[1].wait_recv()
    w_core(2).start()
    pass_on(1, 1)
    w_core(0).wait_recv()
    multiply(0)
    pass_on(2, 0)
    multiply(1)
    pass_on(2, 1)
    forward(0)
    pass_on(3, 0)
    multiply(2)
    forward(1)
    pass_on(3, 1)
    multiply(3)
    forward(2)
    z_copy(0, 4, 0).wait_recv()
    z_copy(1, 4, 1).wait_recv()
    multiply(4)
    forward(3)
    forward(4)

    for n in range(1, 5):
        zz = (z + n) % 4
        rows = pl.ds(pl.multiple_of(zz * REQ, REQ), REQ)
        for core in range(2):
            for k in range(4):
                pltpu.make_async_copy(
                    db.at[0, 0], eb.at[k, core, zz], e_recv.at[k, core, zz]
                ).wait()
        for core in range(2):
            total = eb[0, core, zz].astype(F32)
            for k in range(1, 4):
                total = total + eb[k, core, zz].astype(F32)
            for pair in range(2):
                for step in range(2):
                    parts = [total[at : at + 8] for at in (pair * 16 + step * 8, 32 + pair * 16 + step * 8)]
                    out_ref[4 * pair + 2 * core + step, rows, :] = (
                        jnp.concatenate(parts, axis=0).astype(BF16)
                    )

    for copy in w_right + w_left + w_far:
        copy.wait_send()
    for slot in range(4):
        w_core(slot).wait_send()
    for q in range(2):
        for offset in (1, 2, 3):
            x_copy(q, offset).wait_send()

        @pl.when(t // 4 != q)
        def _():
            x_copy(q, 0).wait_send()

    for dx in (1, 2, 3):
        y_copy(dx).wait_send()

    for d in range(1, 5):
        for half in range(2):
            for way in range(2):
                if d < 4 or half == way:
                    z_copy(way, d, half).wait_send()
    for stage in range(5):
        for i in (1, 2, 3):
            p_copy(stage, i).wait_send()
    for pos in range(8):
        for k in (1, 2, 3):
            e_copy(pos, k).wait_send()

        @pl.when(z_of(pos) // 4 != c)
        def _():
            e_copy(pos, 0).wait_send()


def body(
    query, new_keys, new_values, cache_keys, cache_values, cache_lengths, weight_codes, group_scales
):
    hbm = pl.BlockSpec(memory_space=pl.ANY)
    dma = pltpu.SemaphoreType.DMA
    return pl.pallas_call(
        kernel,
        out_shape=jax.ShapeDtypeStruct((STEPS, 64, 256), BF16),
        in_specs=[pl.BlockSpec(memory_space=pltpu.SMEM)] + [hbm] * 7,
        out_specs=pl.BlockSpec(memory_space=pltpu.VMEM),
        scratch_shapes=[
            pltpu.VMEM((STEPS, REQ, 1024), BF16),
            pltpu.VMEM((STEPS, REQ, HD), BF16),
            pltpu.VMEM((STEPS, REQ, HD), BF16),
            pltpu.VMEM((REQ, CACHE, HD), BF16),
            pltpu.VMEM((REQ, CACHE, HD), BF16),
            pltpu.VMEM((1024, 256), jnp.int32),
            pltpu.VMEM((8, 256), F32),
            pltpu.VMEM((64 * REQ, HD), F32),
            pltpu.VMEM((STEPS * REQ, HD), F32),
            pltpu.VMEM((STEPS * REQ, HD), F32),
            pltpu.VMEM((2, 32 * REQ, HD), F32),
            pltpu.VMEM((8, REQ, 1024), BF16),
            pltpu.VMEM((8, REQ, 1024), BF16),
            pltpu.VMEM((8, 8 * REQ, HD), F32),
            pltpu.VMEM((NX, 2, REQ, 1024), BF16),
            pltpu.VMEM((2, NY, 1024, 256), BF16),
            pltpu.VMEM((8, 4, 2, REQ, 1024), BF16),
            pltpu.VMEM((NY, 8, 64, 256), BF16),
            pltpu.VMEM((NY, 8, 64, 256), BF16),
            pltpu.VMEM((NX, 2, 4, 64, 256), BF16),
            dma((5,)),
            dma((REQ,)),
            dma((REQ,)),
            dma((6,)),
            dma((6,)),
            dma((4,)),
            dma((4,)),
            dma((2, 4)),
            dma((8,)),
            dma((4,)),
            dma((4,)),
            dma((2, 4, 2)),
            dma((2, 4, 2)),
            dma((5, 4)),
            dma((5, 4)),
            dma((NX, 8)),
            dma((NX, 2, 4)),
        ],
        compiler_params=pltpu.CompilerParams(
            collective_id=0, has_side_effects=True, vmem_limit_bytes=60 << 20
        ),
        name="decode",
    )(
        cache_lengths,
        query,
        new_keys,
        new_values,
        cache_keys,
        cache_values,
        weight_codes,
        group_scales,
    )


def solution(mesh):
    return jax.shard_map(
        body,
        mesh=mesh,
        in_specs=(
            P(None, "dp", "tensor"),
            P(None, "dp", "tensor"),
            P(None, "dp", "tensor"),
            P("dp", "tensor", None, None),
            P("dp", "tensor", None, None),
            P("dp"),
            P("tensor", "dp"),
            P("tensor", "dp"),
        ),
        out_specs=P(None, "tensor", "dp"),
        check_vma=False,
    )
```

```python
import functools

import jax
import jax.numpy as jnp
from jax import lax
from jax.experimental import pallas as pl
from jax.experimental.pallas import tpu as pltpu
from jax.sharding import PartitionSpec as P

MESH = pl.DeviceIdType.MESH
HEADS = 64
KVH = 8
HD = 128
D = 8192
GROUP = 128
STEPS = 8
REQ = 16
CACHE = 1024
NX, NY, NZ = 4, 4, 8
GROUPED = 4
LOG2E = 1.4426950408889634
F32 = jnp.float32
BF16 = jnp.bfloat16


def hadamard(size):
    a = lax.broadcasted_iota(jnp.int32, (size, size), 0)
    b = lax.broadcasted_iota(jnp.int32, (size, size), 1)
    bits = a & b
    bits = bits ^ (bits >> 4)
    bits = bits ^ (bits >> 2)
    bits = bits ^ (bits >> 1)
    return (1 - 2 * (bits & 1)).astype(F32)


def butterfly(values):
    span = 1
    while span < len(values):
        out = list(values)
        for at in range(len(values)):
            if at & span == 0:
                out[at] = values[at] + values[at | span]
                out[at | span] = values[at] - values[at | span]
        values = out
        span *= 2
    return values


def kernel(
    lengths,
    q_hbm,
    nk_hbm,
    nv_hbm,
    k_hbm,
    v_hbm,
    codes_hbm,
    scales_hbm,
    out_ref,
    qb,
    nkb,
    nvb,
    kb,
    vb,
    cb,
    sb,
    qf,
    nkf,
    nvf,
    attf,
    att,
    xb,
    rf,
    yb,
    wb,
    ab,
    pb,
    db,
    eb,
    outf,
    load_sem,
    k_sem,
    v_sem,
    w_send,
    w_recv,
    wc_send,
    wc_recv,
    x_send,
    x_recv,
    y_send,
    y_recv,
    z_send,
    z_recv,
    p_send,
    p_recv,
    e_send,
    e_recv,
):
    dp = lax.axis_index("dp")
    t = lax.axis_index("tensor")
    x, c = t // 2, t % 2
    y, z = dp // NZ, dp % NZ

    def device(dx=0, core=None, dy=0, dz=0):
        at_x = (x + dx) % NX
        at_c = c if core is None else core
        return (((y + dy) % NY) * NZ + (z + dz) % NZ, at_x * 2 + at_c)

    def peer(offset):
        return (dp, (t + offset) % 8)

    def remote(src, dst, send, recv, to):
        return pltpu.make_async_remote_copy(
            src_ref=src, dst_ref=dst, send_sem=send, recv_sem=recv, device_id=to, device_id_type=MESH
        )

    barrier = pltpu.get_barrier_semaphore()
    partners = (
        [peer(offset) for offset in range(1, 8)]
        + [device(dy=dy) for dy in (1, 2, 3)]
        + [device(dz=dz) for dz in (1, NZ - 1)]
    )
    for to in partners:
        pl.semaphore_signal(barrier, inc=1, device_id=to, device_id_type=MESH)

    loads = [
        pltpu.make_async_copy(src, dst, load_sem.at[n])
        for n, (src, dst) in enumerate(
            ((codes_hbm, cb), (scales_hbm, sb), (q_hbm, qb), (nk_hbm, nkb), (nv_hbm, nvb))
        )
    ]

    def load_k(r):
        return pltpu.make_async_copy(k_hbm.at[r, 0], kb.at[r], k_sem.at[r])

    def load_v(r):
        return pltpu.make_async_copy(v_hbm.at[r, 0], vb.at[r], v_sem.at[r])

    for load in loads:
        load.start()

    def start_loads(r, carry):
        load_k(r).start()
        load_v(r).start()
        return carry


    loads[0].wait()
    loads[1].wait()
    for group in range(8):
        rows = pl.ds(group * GROUP, GROUP)
        wb[c, 0, rows, :] = (cb[rows, :].astype(F32) * sb[group : group + 1, :]).astype(BF16)
    pl.semaphore_wait(barrier, len(partners))

    half_rows = [pl.ds(0, 512), pl.ds(512, 512)]

    def w_copy(n, src_slot, dst_slot, half, dy):
        return remote(
            wb.at[c, src_slot, half_rows[half]],
            wb.at[c, dst_slot, half_rows[half]],
            w_send.at[n],
            w_recv.at[n],
            device(dy=dy),
        )

    w_right = [w_copy(0, 0, 3, 0, 1), w_copy(1, 0, 3, 1, 1)]
    w_left = [w_copy(2, 0, 1, 0, NY - 1), w_copy(3, 0, 1, 1, NY - 1)]
    w_far = [w_copy(4, 3, 2, 0, 1), w_copy(5, 1, 2, 1, NY - 1)]
    w_right[0].start()
    w_left[1].start()
    w_right[1].start()
    w_left[0].start()

    def w_core(slot):
        return remote(
            wb.at[c, slot], wb.at[c, slot], wc_send.at[slot], wc_recv.at[slot], device(core=1 - c)
        )

    w_core(0).start()
    lax.fori_loop(0, REQ, start_loads, 0)

    for load in loads[2:]:
        load.wait()
    for s in range(STEPS):
        for g in range(8):
            qf[pl.ds((s * 8 + g) * REQ, REQ), :] = qb[s, :, g * HD : (g + 1) * HD].astype(F32)
        nkf[pl.ds(s * REQ, REQ), :] = nkb[s].astype(F32)
        nvf[pl.ds(s * REQ, REQ), :] = nvb[s].astype(F32)

    slots = lax.broadcasted_iota(jnp.int32, (64, CACHE), 1)
    new_slot = lax.broadcasted_iota(jnp.int32, (64, HD), 1)
    new_step = lax.broadcasted_iota(jnp.int32, (64, HD), 0) // 8
    seen = new_slot <= new_step
    transposed = (((1,), (1,)), ((), ()))
    rate = LOG2E * HD ** (-0.5)

    def attend(first, count):
        group = [first + n for n in range(count)]
        for r in group:
            load_k(r).wait()
            load_v(r).wait()
        pad = jnp.zeros((HD - STEPS, HD), F32)
        queries = [
            jnp.concatenate(
                [qf[pl.ds(i * 8 * REQ + r, 8, stride=REQ), :] for i in range(8)], axis=0
            ).astype(BF16)
            for r in group
        ]
        fresh_k, fresh_v = (
            [
                jnp.concatenate([ref[pl.ds(r, STEPS, stride=REQ), :], pad], axis=0).astype(BF16)
                for r in group
            ]
            for ref in (nkf, nvf)
        )
        olds = [
            lax.dot_general(query, kb[r], transposed, preferred_element_type=F32)
            for query, r in zip(queries, group)
        ]
        news = [
            lax.dot_general(query, fresh, transposed, preferred_element_type=F32)
            for query, fresh in zip(queries, fresh_k)
        ]
        results = []
        for n, r in enumerate(group):
            old = jnp.where(slots < lengths[r], olds[n], -1e30)
            new = jnp.where(seen, news[n], -1e30)
            peak = jnp.maximum(
                jnp.max(old, axis=1, keepdims=True), jnp.max(new, axis=1, keepdims=True)
            )
            old = jnp.exp2((old - peak) * rate)
            new = jnp.exp2((new - peak) * rate)
            total = jnp.sum(old, axis=1, keepdims=True) + jnp.sum(new, axis=1, keepdims=True)
            result = jnp.dot(old.astype(BF16), vb[r], preferred_element_type=F32)
            result = result + jnp.dot(new.astype(BF16), fresh_v[n], preferred_element_type=F32)
            results.append(result / total)
        for r, result in zip(group, results):
            for i in range(8):
                start = (i // 2) * 8 * REQ + (i % 2) * 8 + r % 8
                attf[r // 8, pl.ds(start, 8, stride=REQ), :] = result[i * 8 : (i + 1) * 8, :]

    def attend_some(n, carry):
        attend(GROUPED * n, GROUPED)
        return carry

    def x_copy(q, offset):
        to = 2 * ((x + offset) % NX) + q
        return remote(att.at[to], xb.at[t], x_send.at[q, offset], x_recv.at[t], (dp, to))

    def x_local():
        return pltpu.make_async_copy(att.at[t], xb.at[t], x_recv.at[t])

    for q in range(2):
        lax.fori_loop(q * 8 // GROUPED, (q + 1) * 8 // GROUPED, attend_some, 0)
        for u in range(4):
            for g in range(8):
                att[2 * u + q, :, g * HD : (g + 1) * HD] = attf[
                    q, pl.ds((u * 8 + g) * REQ, REQ), :
                ].astype(BF16)
        for offset in (2, 1, 3):
            x_copy(q, offset).start()

        @pl.when(c == q)
        def _():
            x_local().start()

        @pl.when(c != q)
        def _():
            x_copy(q, 0).start()

    w_right[0].wait_recv()
    w_far[0].start()
    w_left[1].wait_recv()
    w_far[1].start()

    for source in range(8):
        pltpu.make_async_copy(att.at[0], xb.at[source], x_recv.at[source]).wait()

    signs = hadamard(HD).astype(BF16)
    for g in range(8):
        heads = xb[:, :, g * HD : (g + 1) * HD].reshape(8 * REQ, HD)
        rf[g] = jnp.dot(heads, signs, preferred_element_type=F32)
    for kv in range(8):
        rows = pl.ds(kv * REQ, REQ)
        for g, value in enumerate(butterfly([rf[g, rows, :] for g in range(8)])):
            rf[g, rows, :] = value
    top = jnp.zeros((REQ, HD), F32)
    for g in range(8):
        values = butterfly([rf[g, pl.ds(kv * REQ, REQ), :] for kv in range(8)])
        for kv, value in enumerate(values):
            value = (value * D ** (-0.5)).astype(BF16)
            yb[kv // 2, kv % 2, :, g * HD : (g + 1) * HD] = value
            top = jnp.maximum(top, jnp.abs(value.astype(F32)))
    limit = 0.9 * jnp.max(top, axis=1, keepdims=True)
    for kv in range(8):
        value = yb[kv // 2, kv % 2].astype(F32)
        yb[kv // 2, kv % 2] = jnp.clip(value, -limit, limit).astype(BF16)

    def y_copy(dx):
        return remote(
            yb.at[(x + dx) % NX], ab.at[0, dx], y_send.at[dx], y_recv.at[dx], device(dx=dx)
        )

    def z_copy(way, d, k):
        src = 0 if d == 1 else (2 * (d - 1) - 1 if way == 0 else 2 * (d - 1))
        dst = 7 if d == 4 else (2 * d - 1 if way == 0 else 2 * d)
        return remote(
            ab.at[src, k],
            ab.at[dst, k],
            z_send.at[way, d - 1, k],
            z_recv.at[way, d - 1, k],
            device(dz=1 if way == 0 else NZ - 1),
        )

    def goes(way, d, k):
        return d < 4 or k // 2 == way

    def z_first(k):
        if k:
            y_copy(k).wait_recv()
        for way in range(2):
            z_copy(way, 1, k).start()

    ab[0, 0] = yb[x]
    z_first(0)
    for dx in (1, 3, 2):
        y_copy(dx).start()

    spans = [(0, 1), (1, 3), (3, 5), (5, 7), (7, 8)]

    def slots_of(part):
        return (0, 4) if part is None else (2 * part, 2 * part + 2)

    def project(stage, part, i):
        lo, hi = spans[stage]
        first, last = slots_of(part)
        rows = (hi - lo) * (last - first) * REQ
        total = jnp.zeros((rows, 256), F32)
        for core in range(2):
            block = ab[lo:hi, first:last, core].reshape(rows, 1024)
            total = total + jnp.dot(block, wb[core, i], preferred_element_type=F32)
        total = total.astype(BF16).reshape(hi - lo, (last - first) * REQ, 256)
        to = pb if i else db
        to[i, lo:hi, first * REQ : last * REQ] = total

    def p_copy(stage, part, i):
        lo, hi = spans[stage]
        first, last = slots_of(part)
        at = (i, pl.ds(lo, hi - lo), pl.ds(first * REQ, (last - first) * REQ))
        n = part or 0
        return remote(
            pb.at[at], db.at[at], p_send.at[stage, n, i], p_recv.at[stage, n, i], device(dy=i)
        )

    def z_of(pos):
        dz = 4 if pos == 7 else (NZ - (pos + 1) // 2 if pos % 2 else pos // 2)
        return (z + dz) % NZ

    def e_copy(pos, part, k):
        block = z_of(pos)
        to_x = (x + k) % NX
        i = (y + NY - to_x) % NY
        first, last = slots_of(part)
        rows = pl.ds(first * REQ, (last - first) * REQ)
        return remote(
            db.at[i, pos, rows],
            eb.at[k, c, block % 4, rows],
            e_send.at[k, pos, part or 0],
            e_recv.at[k, c, block % 4],
            device(dx=k, core=block // 4),
        )

    def e_local(pos, part):
        block = z_of(pos)
        i = (y + NY - x) % NY
        first, last = slots_of(part)
        rows = pl.ds(first * REQ, (last - first) * REQ)
        return pltpu.make_async_copy(
            db.at[i, pos, rows], eb.at[0, c, block % 4, rows], e_recv.at[0, c, block % 4]
        )

    def p_arrived(stage, part):
        for i in (1, 3, 2):
            p_copy(stage, part, i).wait_recv()

    def forward(stage, part):
        for pos in range(*spans[stage]):
            for k in (2, 1, 3):
                e_copy(pos, part, k).start()
            own = z_of(pos) // 4 == c

            @pl.when(own)
            def _():
                e_local(pos, part).start()

            @pl.when(jnp.logical_not(own))
            def _():
                e_copy(pos, part, 0).start()

    def pass_on(d, k):
        for way in range(2):
            z_copy(way, d, k).wait_recv()
            if goes(way, d + 1, k):
                z_copy(way, d + 1, k).start()

    def multiply(stage, part):
        for i in (2, 1, 3, 0):
            project(stage, part, i)
            if i:
                p_copy(stage, part, i).start()

    z_first(1)
    w_right[1].wait_recv()
    w_core(3).start()
    w_left[0].wait_recv()
    w_core(1).start()
    pass_on(1, 0)
    z_first(3)
    z_first(2)
    pass_on(1, 1)
    pass_on(1, 3)
    w_far[0].wait_recv()
    w_far[1].wait_recv()
    w_core(2).start()
    for slot in (0, 3, 1):
        w_core(slot).wait_recv()
    pass_on(1, 2)
    pass_on(2, 0)
    w_core(2).wait_recv()
    multiply(0, None)
    pass_on(2, 1)
    multiply(1, None)
    pass_on(2, 3)
    pass_on(2, 2)
    pass_on(3, 0)
    multiply(2, None)
    pass_on(3, 1)
    p_arrived(0, None)
    forward(0, None)
    pass_on(3, 3)
    p_arrived(1, None)
    forward(1, None)
    pass_on(3, 2)
    multiply(3, None)
    p_arrived(2, None)
    forward(2, None)
    for k in (0, 1):
        z_copy(0, 4, k).wait_recv()
    for k in (3, 2):
        z_copy(1, 4, k).wait_recv()
    multiply(4, None)
    p_arrived(3, None)
    forward(3, None)
    p_arrived(4, None)
    forward(4, None)

    for n in range(1, 5):
        zz = (z + n) % 4
        for core in range(2):
            for k in range(4):
                pltpu.make_async_copy(
                    db.at[0, 0], eb.at[k, core, zz], e_recv.at[k, core, zz]
                ).wait()
        for core in range(2):
            for m in range(4):
                total = eb[0, core, zz, m * REQ : (m + 1) * REQ, :].astype(F32)
                for k in range(1, 4):
                    slot = (m - k) % 4
                    total = total + eb[k, core, zz, slot * REQ : (slot + 1) * REQ, :].astype(F32)
                source = (x + 4 - m) % 4
                rows = pl.ds(pl.multiple_of(zz * REQ + core * 8, 8), 8)
                outf[2 * source, rows, :] = total[:8]
                outf[2 * source + 1, rows, :] = total[8:]
    for step in range(STEPS):
        out_ref[step] = outf[step].astype(BF16)

    for copy in w_right + w_left + w_far:
        copy.wait_send()
    for slot in range(4):
        w_core(slot).wait_send()
    for q in range(2):
        for offset in (1, 2, 3):
            x_copy(q, offset).wait_send()

        @pl.when(c != q)
        def _():
            x_copy(q, 0).wait_send()

    for dx in (1, 2, 3):
        y_copy(dx).wait_send()

    for d in range(1, 5):
        for k in range(4):
            for way in range(2):
                if goes(way, d, k):
                    z_copy(way, d, k).wait_send()
    for stage in range(5):
        for part in (None,):
            for i in (1, 2, 3):
                p_copy(stage, part, i).wait_send()
        for pos in range(*spans[stage]):
            for part in (None,):
                for k in (1, 2, 3):
                    e_copy(pos, part, k).wait_send()

                @pl.when(z_of(pos) // 4 != c)
                def _():
                    e_copy(pos, part, 0).wait_send()


def body(
    query, new_keys, new_values, cache_keys, cache_values, cache_lengths, weight_codes, group_scales
):
    hbm = pl.BlockSpec(memory_space=pl.ANY)
    dma = pltpu.SemaphoreType.DMA
    return pl.pallas_call(
        kernel,
        out_shape=jax.ShapeDtypeStruct((STEPS, 64, 256), BF16),
        in_specs=[pl.BlockSpec(memory_space=pltpu.SMEM)] + [hbm] * 7,
        out_specs=pl.BlockSpec(memory_space=pltpu.VMEM),
        scratch_shapes=[
            pltpu.VMEM((STEPS, REQ, 1024), BF16),
            pltpu.VMEM((STEPS, REQ, HD), BF16),
            pltpu.VMEM((STEPS, REQ, HD), BF16),
            pltpu.VMEM((REQ, CACHE, HD), BF16),
            pltpu.VMEM((REQ, CACHE, HD), BF16),
            pltpu.VMEM((1024, 256), jnp.int32),
            pltpu.VMEM((8, 256), F32),
            pltpu.VMEM((64 * REQ, HD), F32),
            pltpu.VMEM((STEPS * REQ, HD), F32),
            pltpu.VMEM((STEPS * REQ, HD), F32),
            pltpu.VMEM((2, 32 * REQ, HD), F32),
            pltpu.VMEM((8, REQ, 1024), BF16),
            pltpu.VMEM((8, REQ, 1024), BF16),
            pltpu.VMEM((8, 8 * REQ, HD), F32),
            pltpu.VMEM((NX, 2, REQ, 1024), BF16),
            pltpu.VMEM((2, NY, 1024, 256), BF16),
            pltpu.VMEM((8, 4, 2, REQ, 1024), BF16),
            pltpu.VMEM((NY, 8, 64, 256), BF16),
            pltpu.VMEM((NY, 8, 64, 256), BF16),
            pltpu.VMEM((NX, 2, 4, 64, 256), BF16),
            pltpu.VMEM((STEPS, 64, 256), F32),
            dma((5,)),
            dma((REQ,)),
            dma((REQ,)),
            dma((6,)),
            dma((6,)),
            dma((4,)),
            dma((4,)),
            dma((2, 4)),
            dma((8,)),
            dma((4,)),
            dma((4,)),
            dma((2, 4, 4)),
            dma((2, 4, 4)),
            dma((5, 2, 4)),
            dma((5, 2, 4)),
            dma((NX, 8, 2)),
            dma((NX, 2, 4)),
        ],
        compiler_params=pltpu.CompilerParams(
            collective_id=0, has_side_effects=True, vmem_limit_bytes=60 << 20
        ),
        name="decode",
    )(
        cache_lengths,
        query,
        new_keys,
        new_values,
        cache_keys,
        cache_values,
        weight_codes,
        group_scales,
    )


def solution(mesh):
    return jax.shard_map(
        body,
        mesh=mesh,
        in_specs=(
            P(None, "dp", "tensor"),
            P(None, "dp", "tensor"),
            P(None, "dp", "tensor"),
            P("dp", "tensor", None, None),
            P("dp", "tensor", None, None),
            P("dp"),
            P("tensor", "dp"),
            P("tensor", "dp"),
        ),
        out_specs=P(None, "tensor", "dp"),
        check_vma=False,
    )
```

```python
import functools

import jax
import jax.numpy as jnp
from jax import lax
from jax.experimental import pallas as pl
from jax.experimental.pallas import tpu as pltpu
from jax.sharding import PartitionSpec as P

MESH = pl.DeviceIdType.MESH
HEADS = 64
KVH = 8
HD = 128
D = 8192
GROUP = 128
STEPS = 8
REQ = 16
CACHE = 1024
NX, NY, NZ = 4, 4, 8
GROUPED = 4
LOG2E = 1.4426950408889634
F32 = jnp.float32
BF16 = jnp.bfloat16


def hadamard(size):
    a = lax.broadcasted_iota(jnp.int32, (size, size), 0)
    b = lax.broadcasted_iota(jnp.int32, (size, size), 1)
    bits = a & b
    bits = bits ^ (bits >> 4)
    bits = bits ^ (bits >> 2)
    bits = bits ^ (bits >> 1)
    return (1 - 2 * (bits & 1)).astype(F32)


def butterfly(values):
    span = 1
    while span < len(values):
        out = list(values)
        for at in range(len(values)):
            if at & span == 0:
                out[at] = values[at] + values[at | span]
                out[at | span] = values[at] - values[at | span]
        values = out
        span *= 2
    return values


def kernel(
    lengths,
    q_hbm,
    nk_hbm,
    nv_hbm,
    k_hbm,
    v_hbm,
    codes_hbm,
    scales_hbm,
    out_ref,
    qb,
    nkb,
    nvb,
    kb,
    vb,
    cb,
    sb,
    qf,
    nkf,
    nvf,
    attf,
    att,
    xb,
    rf,
    yb,
    wb,
    ab,
    pb,
    db,
    eb,
    outf,
    load_sem,
    k_sem,
    v_sem,
    w_send,
    w_recv,
    wc_send,
    wc_recv,
    x_send,
    x_recv,
    y_send,
    y_recv,
    z_send,
    z_recv,
    p_send,
    p_recv,
    e_send,
    e_recv,
):
    dp = lax.axis_index("dp")
    t = lax.axis_index("tensor")
    x, c = t // 2, t % 2
    y, z = dp // NZ, dp % NZ

    def device(dx=0, core=None, dy=0, dz=0):
        at_x = (x + dx) % NX
        at_c = c if core is None else core
        return (((y + dy) % NY) * NZ + (z + dz) % NZ, at_x * 2 + at_c)

    def peer(offset):
        return (dp, (t + offset) % 8)

    def remote(src, dst, send, recv, to):
        return pltpu.make_async_remote_copy(
            src_ref=src, dst_ref=dst, send_sem=send, recv_sem=recv, device_id=to, device_id_type=MESH
        )

    barrier = pltpu.get_barrier_semaphore()
    partners = (
        [peer(offset) for offset in range(1, 8)]
        + [device(dy=dy) for dy in (1, 2, 3)]
        + [device(dz=dz) for dz in (1, NZ - 1)]
    )
    for to in partners:
        pl.semaphore_signal(barrier, inc=1, device_id=to, device_id_type=MESH)

    loads = [
        pltpu.make_async_copy(src, dst, load_sem.at[n])
        for n, (src, dst) in enumerate(
            ((codes_hbm, cb), (scales_hbm, sb), (q_hbm, qb), (nk_hbm, nkb), (nv_hbm, nvb))
        )
    ]

    def load_k(r):
        return pltpu.make_async_copy(k_hbm.at[r, 0], kb.at[r], k_sem.at[r])

    def load_v(r):
        return pltpu.make_async_copy(v_hbm.at[r, 0], vb.at[r], v_sem.at[r])

    for load in loads:
        load.start()

    def start_loads(r, carry):
        load_k(r).start()
        load_v(r).start()
        return carry


    loads[0].wait()
    loads[1].wait()
    for group in range(8):
        rows = pl.ds(group * GROUP, GROUP)
        wb[c, 0, rows, :] = (cb[rows, :].astype(F32) * sb[group : group + 1, :]).astype(BF16)
    pl.semaphore_wait(barrier, len(partners))

    half_rows = [pl.ds(0, 512), pl.ds(512, 512)]

    def w_copy(n, src_slot, dst_slot, half, dy):
        return remote(
            wb.at[c, src_slot, half_rows[half]],
            wb.at[c, dst_slot, half_rows[half]],
            w_send.at[n],
            w_recv.at[n],
            device(dy=dy),
        )

    w_right = [w_copy(0, 0, 3, 0, 1), w_copy(1, 0, 3, 1, 1)]
    w_left = [w_copy(2, 0, 1, 0, NY - 1), w_copy(3, 0, 1, 1, NY - 1)]
    w_far = [w_copy(4, 3, 2, 0, 1), w_copy(5, 1, 2, 1, NY - 1)]
    w_right[0].start()
    w_left[1].start()
    w_right[1].start()
    w_left[0].start()

    def w_core(slot):
        return remote(
            wb.at[c, slot], wb.at[c, slot], wc_send.at[slot], wc_recv.at[slot], device(core=1 - c)
        )

    w_core(0).start()
    lax.fori_loop(0, REQ, start_loads, 0)

    for load in loads[2:]:
        load.wait()
    for s in range(STEPS):
        for g in range(8):
            qf[pl.ds((s * 8 + g) * REQ, REQ), :] = qb[s, :, g * HD : (g + 1) * HD].astype(F32)
        nkf[pl.ds(s * REQ, REQ), :] = nkb[s].astype(F32)
        nvf[pl.ds(s * REQ, REQ), :] = nvb[s].astype(F32)

    slots = lax.broadcasted_iota(jnp.int32, (64, CACHE), 1)
    new_slot = lax.broadcasted_iota(jnp.int32, (64, HD), 1)
    new_step = lax.broadcasted_iota(jnp.int32, (64, HD), 0) // 8
    seen = new_slot <= new_step
    transposed = (((1,), (1,)), ((), ()))
    rate = LOG2E * HD ** (-0.5)

    def attend(first, count):
        group = [first + n for n in range(count)]
        for r in group:
            load_k(r).wait()
            load_v(r).wait()
        pad = jnp.zeros((HD - STEPS, HD), F32)
        queries = [
            jnp.concatenate(
                [qf[pl.ds(i * 8 * REQ + r, 8, stride=REQ), :] for i in range(8)], axis=0
            ).astype(BF16)
            for r in group
        ]
        fresh_k, fresh_v = (
            [
                jnp.concatenate([ref[pl.ds(r, STEPS, stride=REQ), :], pad], axis=0).astype(BF16)
                for r in group
            ]
            for ref in (nkf, nvf)
        )
        olds = [
            lax.dot_general(query, kb[r], transposed, preferred_element_type=F32)
            for query, r in zip(queries, group)
        ]
        news = [
            lax.dot_general(query, fresh, transposed, preferred_element_type=F32)
            for query, fresh in zip(queries, fresh_k)
        ]
        results = []
        for n, r in enumerate(group):
            old = jnp.where(slots < lengths[r], olds[n], -1e30)
            new = jnp.where(seen, news[n], -1e30)
            peak = jnp.maximum(
                jnp.max(old, axis=1, keepdims=True), jnp.max(new, axis=1, keepdims=True)
            )
            old = jnp.exp2((old - peak) * rate)
            new = jnp.exp2((new - peak) * rate)
            total = jnp.sum(old, axis=1, keepdims=True) + jnp.sum(new, axis=1, keepdims=True)
            result = jnp.dot(old.astype(BF16), vb[r], preferred_element_type=F32)
            result = result + jnp.dot(new.astype(BF16), fresh_v[n], preferred_element_type=F32)
            results.append(result / total)
        for r, result in zip(group, results):
            for i in range(8):
                start = (i // 2) * 8 * REQ + (i % 2) * 8 + r % 8
                attf[r // 8, pl.ds(start, 8, stride=REQ), :] = result[i * 8 : (i + 1) * 8, :]

    def attend_some(n, carry):
        attend(GROUPED * n, GROUPED)
        return carry

    def x_copy(q, offset):
        to = 2 * ((x + offset) % NX) + q
        return remote(att.at[to], xb.at[t], x_send.at[q, offset], x_recv.at[t], (dp, to))

    def x_local():
        return pltpu.make_async_copy(att.at[t], xb.at[t], x_recv.at[t])

    for q in range(2):
        lax.fori_loop(q * 8 // GROUPED, (q + 1) * 8 // GROUPED, attend_some, 0)
        for u in range(4):
            for g in range(8):
                att[2 * u + q, :, g * HD : (g + 1) * HD] = attf[
                    q, pl.ds((u * 8 + g) * REQ, REQ), :
                ].astype(BF16)
        for offset in (2, 1, 3):
            x_copy(q, offset).start()

        @pl.when(c == q)
        def _():
            x_local().start()

        @pl.when(c != q)
        def _():
            x_copy(q, 0).start()

    w_right[0].wait_recv()
    w_far[0].start()
    w_left[1].wait_recv()
    w_far[1].start()

    for source in range(8):
        pltpu.make_async_copy(att.at[0], xb.at[source], x_recv.at[source]).wait()

    signs = hadamard(HD).astype(BF16)
    for g in range(8):
        heads = xb[:, :, g * HD : (g + 1) * HD].reshape(8 * REQ, HD)
        rf[g] = jnp.dot(heads, signs, preferred_element_type=F32)
    for kv in range(8):
        rows = pl.ds(kv * REQ, REQ)
        for g, value in enumerate(butterfly([rf[g, rows, :] for g in range(8)])):
            rf[g, rows, :] = value
    top = jnp.zeros((REQ, HD), F32)
    for g in range(8):
        values = butterfly([rf[g, pl.ds(kv * REQ, REQ), :] for kv in range(8)])
        for kv, value in enumerate(values):
            value = (value * D ** (-0.5)).astype(BF16)
            yb[kv // 2, kv % 2, :, g * HD : (g + 1) * HD] = value
            top = jnp.maximum(top, jnp.abs(value.astype(F32)))
    limit = 0.9 * jnp.max(top, axis=1, keepdims=True)
    for kv in range(8):
        value = yb[kv // 2, kv % 2].astype(F32)
        yb[kv // 2, kv % 2] = jnp.clip(value, -limit, limit).astype(BF16)

    def y_copy(dx):
        return remote(
            yb.at[(x + dx) % NX], ab.at[0, dx], y_send.at[dx], y_recv.at[dx], device(dx=dx)
        )

    def z_copy(way, d, k):
        src = 0 if d == 1 else (2 * (d - 1) - 1 if way == 0 else 2 * (d - 1))
        dst = 7 if d == 4 else (2 * d - 1 if way == 0 else 2 * d)
        return remote(
            ab.at[src, k],
            ab.at[dst, k],
            z_send.at[way, d - 1, k],
            z_recv.at[way, d - 1, k],
            device(dz=1 if way == 0 else NZ - 1),
        )

    def goes(way, d, k):
        return d < 4 or k // 2 == way

    def z_first(k):
        if k:
            y_copy(k).wait_recv()
        for way in range(2):
            z_copy(way, 1, k).start()

    ab[0, 0] = yb[x]
    z_first(0)
    for dx in (1, 3, 2):
        y_copy(dx).start()

    spans = [(0, 1), (1, 3), (3, 5), (5, 7), (7, 8)]

    def slots_of(part):
        return (0, 4) if part is None else (2 * part, 2 * part + 2)

    def project(stage, part, i):
        lo, hi = spans[stage]
        first, last = slots_of(part)
        rows = (hi - lo) * (last - first) * REQ
        total = jnp.zeros((rows, 256), F32)
        for core in range(2):
            block = ab[lo:hi, first:last, core].reshape(rows, 1024)
            total = total + jnp.dot(block, wb[core, i], preferred_element_type=F32)
        total = total.astype(BF16).reshape(hi - lo, (last - first) * REQ, 256)
        to = pb if i else db
        to[i, lo:hi, first * REQ : last * REQ] = total

    def p_copy(stage, part, i):
        lo, hi = spans[stage]
        first, last = slots_of(part)
        at = (i, pl.ds(lo, hi - lo), pl.ds(first * REQ, (last - first) * REQ))
        n = part or 0
        return remote(
            pb.at[at], db.at[at], p_send.at[stage, n, i], p_recv.at[stage, n, i], device(dy=i)
        )

    def z_of(pos):
        dz = 4 if pos == 7 else (NZ - (pos + 1) // 2 if pos % 2 else pos // 2)
        return (z + dz) % NZ

    def e_copy(pos, part, k):
        block = z_of(pos)
        to_x = (x + k) % NX
        i = (y + NY - to_x) % NY
        first, last = slots_of(part)
        rows = pl.ds(first * REQ, (last - first) * REQ)
        return remote(
            db.at[i, pos, rows],
            eb.at[k, c, block % 4, rows],
            e_send.at[k, pos, part or 0],
            e_recv.at[k, c, block % 4],
            device(dx=k, core=block // 4),
        )

    def e_local(pos, part):
        block = z_of(pos)
        i = (y + NY - x) % NY
        first, last = slots_of(part)
        rows = pl.ds(first * REQ, (last - first) * REQ)
        return pltpu.make_async_copy(
            db.at[i, pos, rows], eb.at[0, c, block % 4, rows], e_recv.at[0, c, block % 4]
        )

    def p_arrived(stage, part):
        for i in (1, 3, 2):
            p_copy(stage, part, i).wait_recv()

    def forward(stage, part):
        for pos in range(*spans[stage]):
            for k in (2, 1, 3):
                e_copy(pos, part, k).start()
            own = z_of(pos) // 4 == c

            @pl.when(own)
            def _():
                e_local(pos, part).start()

            @pl.when(jnp.logical_not(own))
            def _():
                e_copy(pos, part, 0).start()

    def pass_on(d, k):
        for way in range(2):
            z_copy(way, d, k).wait_recv()
            if goes(way, d + 1, k):
                z_copy(way, d + 1, k).start()

    def multiply(stage, part):
        for i in (2, 1, 3, 0):
            project(stage, part, i)
            if i:
                p_copy(stage, part, i).start()

    z_first(1)
    w_right[1].wait_recv()
    w_core(3).start()
    w_left[0].wait_recv()
    w_core(1).start()
    pass_on(1, 0)
    z_first(3)
    z_first(2)
    pass_on(1, 1)
    pass_on(1, 3)
    w_far[0].wait_recv()
    w_far[1].wait_recv()
    w_core(2).start()
    for slot in (0, 3, 1):
        w_core(slot).wait_recv()
    pass_on(1, 2)
    pass_on(2, 0)
    w_core(2).wait_recv()
    multiply(0, None)
    pass_on(2, 1)
    multiply(1, None)
    pass_on(2, 3)
    pass_on(2, 2)
    multiply(2, None)
    pass_on(3, 0)
    p_arrived(0, None)
    forward(0, None)
    pass_on(3, 1)
    p_arrived(1, None)
    forward(1, None)
    pass_on(3, 3)
    pass_on(3, 2)
    multiply(3, None)
    p_arrived(2, None)
    forward(2, None)
    for k in (0, 1):
        z_copy(0, 4, k).wait_recv()
    for k in (3, 2):
        z_copy(1, 4, k).wait_recv()
    multiply(4, None)
    p_arrived(3, None)
    forward(3, None)
    p_arrived(4, None)
    forward(4, None)

    for n in range(1, 5):
        zz = (z + n) % 4
        for core in range(2):
            for k in range(4):
                pltpu.make_async_copy(
                    db.at[0, 0], eb.at[k, core, zz], e_recv.at[k, core, zz]
                ).wait()
        for core in range(2):
            for m in range(4):
                total = eb[0, core, zz, m * REQ : (m + 1) * REQ, :].astype(F32)
                for k in range(1, 4):
                    slot = (m - k) % 4
                    total = total + eb[k, core, zz, slot * REQ : (slot + 1) * REQ, :].astype(F32)
                source = (x + 4 - m) % 4
                rows = pl.ds(pl.multiple_of(zz * REQ + core * 8, 8), 8)
                outf[2 * source, rows, :] = total[:8]
                outf[2 * source + 1, rows, :] = total[8:]
    for step in range(STEPS):
        out_ref[step] = outf[step].astype(BF16)

    for copy in w_right + w_left + w_far:
        copy.wait_send()
    for slot in range(4):
        w_core(slot).wait_send()
    for q in range(2):
        for offset in (1, 2, 3):
            x_copy(q, offset).wait_send()

        @pl.when(c != q)
        def _():
            x_copy(q, 0).wait_send()

    for dx in (1, 2, 3):
        y_copy(dx).wait_send()

    for d in range(1, 5):
        for k in range(4):
            for way in range(2):
                if goes(way, d, k):
                    z_copy(way, d, k).wait_send()
    for stage in range(5):
        for part in (None,):
            for i in (1, 2, 3):
                p_copy(stage, part, i).wait_send()
        for pos in range(*spans[stage]):
            for part in (None,):
                for k in (1, 2, 3):
                    e_copy(pos, part, k).wait_send()

                @pl.when(z_of(pos) // 4 != c)
                def _():
                    e_copy(pos, part, 0).wait_send()


def body(
    query, new_keys, new_values, cache_keys, cache_values, cache_lengths, weight_codes, group_scales
):
    hbm = pl.BlockSpec(memory_space=pl.ANY)
    dma = pltpu.SemaphoreType.DMA
    return pl.pallas_call(
        kernel,
        out_shape=jax.ShapeDtypeStruct((STEPS, 64, 256), BF16),
        in_specs=[pl.BlockSpec(memory_space=pltpu.SMEM)] + [hbm] * 7,
        out_specs=pl.BlockSpec(memory_space=pltpu.VMEM),
        scratch_shapes=[
            pltpu.VMEM((STEPS, REQ, 1024), BF16),
            pltpu.VMEM((STEPS, REQ, HD), BF16),
            pltpu.VMEM((STEPS, REQ, HD), BF16),
            pltpu.VMEM((REQ, CACHE, HD), BF16),
            pltpu.VMEM((REQ, CACHE, HD), BF16),
            pltpu.VMEM((1024, 256), jnp.int32),
            pltpu.VMEM((8, 256), F32),
            pltpu.VMEM((64 * REQ, HD), F32),
            pltpu.VMEM((STEPS * REQ, HD), F32),
            pltpu.VMEM((STEPS * REQ, HD), F32),
            pltpu.VMEM((2, 32 * REQ, HD), F32),
            pltpu.VMEM((8, REQ, 1024), BF16),
            pltpu.VMEM((8, REQ, 1024), BF16),
            pltpu.VMEM((8, 8 * REQ, HD), F32),
            pltpu.VMEM((NX, 2, REQ, 1024), BF16),
            pltpu.VMEM((2, NY, 1024, 256), BF16),
            pltpu.VMEM((8, 4, 2, REQ, 1024), BF16),
            pltpu.VMEM((NY, 8, 64, 256), BF16),
            pltpu.VMEM((NY, 8, 64, 256), BF16),
            pltpu.VMEM((NX, 2, 4, 64, 256), BF16),
            pltpu.VMEM((STEPS, 64, 256), F32),
            dma((5,)),
            dma((REQ,)),
            dma((REQ,)),
            dma((6,)),
            dma((6,)),
            dma((4,)),
            dma((4,)),
            dma((2, 4)),
            dma((8,)),
            dma((4,)),
            dma((4,)),
            dma((2, 4, 4)),
            dma((2, 4, 4)),
            dma((5, 2, 4)),
            dma((5, 2, 4)),
            dma((NX, 8, 2)),
            dma((NX, 2, 4)),
        ],
        compiler_params=pltpu.CompilerParams(
            collective_id=0, has_side_effects=True, vmem_limit_bytes=60 << 20
        ),
        name="decode",
    )(
        cache_lengths,
        query,
        new_keys,
        new_values,
        cache_keys,
        cache_values,
        weight_codes,
        group_scales,
    )


def solution(mesh):
    return jax.shard_map(
        body,
        mesh=mesh,
        in_specs=(
            P(None, "dp", "tensor"),
            P(None, "dp", "tensor"),
            P(None, "dp", "tensor"),
            P("dp", "tensor", None, None),
            P("dp", "tensor", None, None),
            P("dp"),
            P("tensor", "dp"),
            P("tensor", "dp"),
        ),
        out_specs=P(None, "tensor", "dp"),
        check_vma=False,
    )
```
